32 devices in a mesh: batch: 4 (over y, core), group: 2 (over x), ctx: 4 (over z).
Axes of the slice: x: 2, y: 2, z: 4, core: 2. Of those that a mesh axis runs over, the one named last changes fastest.
Arguments:
- block_input: bfloat16 [16, 2048, 1024], P(('batch', 'group'), 'ctx'), may hold values from -6 to 6
- doc_ids: int32 [16, 2048], P(('batch', 'group')), may hold values from 0 to 1, as said below
- out_cotangent: bfloat16 [16, 2048, 1024], P(('batch', 'group'), 'ctx'), may hold values from -6 to 6
- inward_weight: float32 [1024, 3072], P(None, 'group'), may hold values from -0.25 to 0.25
- inward_moment: float32 [1024, 3072], P(None, 'group')
- inward_square: float32 [1024, 3072], P(None, 'group'), as said below
- outward_weight: float32 [1024, 1024], P(None, 'group'), may hold values from -0.75 to 0.75
- outward_moment: float32 [1024, 1024], P(None, 'group')
- outward_square: float32 [1024, 1024], P(None, 'group'), as said below
- expand_weight: float32 [1024, 4096], P(None, 'group'), may hold values from -0.1875 to 0.1875
- expand_moment: float32 [1024, 4096], P(None, 'group')
- expand_square: float32 [1024, 4096], P(None, 'group'), as said below
- shrink_weight: float32 [4096, 1024], P(None, 'group'), may hold values from -0.09375 to 0.09375
- shrink_moment: float32 [4096, 1024], P(None, 'group')
- shrink_square: float32 [4096, 1024], P(None, 'group'), as said below
- vector_weight: float32 [13, 1024], P(None, 'group')
- vector_moment: float32 [13, 1024], P(None, 'group')
- vector_square: float32 [13, 1024], P(None, 'group'), as said below
Outputs:
- block_output: bfloat16 [16, 2048, 1024], P(('batch', 'group'), 'ctx')
- input_grad: float32 [16, 2048, 1024], P(('batch', 'group'), 'ctx')
- inward_master: float32 [1024, 3072], P(None, 'group')
- inward_first: float32 [1024, 3072], P(None, 'group')
- inward_second: float32 [1024, 3072], P(None, 'group')
- outward_master: float32 [1024, 1024], P(None, 'group')
- outward_first: float32 [1024, 1024], P(None, 'group')
- outward_second: float32 [1024, 1024], P(None, 'group')
- expand_master: float32 [1024, 4096], P(None, 'group')
- expand_first: float32 [1024, 4096], P(None, 'group')
- expand_second: float32 [1024, 4096], P(None, 'group')
- shrink_master: float32 [4096, 1024], P(None, 'group')
- shrink_first: float32 [4096, 1024], P(None, 'group')
- shrink_second: float32 [4096, 1024], P(None, 'group')
- vector_master: float32 [13, 1024], P(None, 'group')
- vector_first: float32 [13, 1024], P(None, 'group')
- vector_second: float32 [13, 1024], P(None, 'group')
The draws below stay inside these ranges and needn't reach their ends.
Inputs may be any that keep to these rules, and one draw needn't show every extreme that they name: `doc_ids`: each sequence is document 0 up to a cut and document 1 from it on, both nonempty; in every aligned block of 2 sequences one sequence has its cut within its last 512 positions. `inward_square`: entries are positive. `outward_square`: entries are positive. `expand_square`: entries are positive. `shrink_square`: entries are positive. `vector_square`: entries are positive.
All inputs are finite; a program needn't handle non-finite values.
Results may differ from the reference program's by a relative error of at most 0.012.
The reference program's roundings to bfloat16 on the way count: a program that leaves them out, or rounds other values in their place, can miss the bound.
Values may be sent and summed in bfloat16 or wider, within the bound.
A program may use at most 704 MiB of HBM per device.

```python
import math
import jax
import jax.numpy as jnp
from jax import lax

D = 1024
FF = 4096
HEADS = 16
ROTARY = 16
SEQ_LEN = 2048
SEQ_DEV = 2
STEP = 10
SEQS = 16
TOK_CTX = 512
VEC_ROWS = 13


def gradient_size(factor):
    return factor * math.sqrt(SEQS * SEQ_LEN)


def first_entries(key, shape, factor):
    return jax.random.normal(key, shape, jnp.float32) * (gradient_size(factor) / 9.0)


def second_entries(key, shape, factor):
    spread = jnp.exp(jax.random.uniform(key, shape, jnp.float32, math.log(0.5), math.log(8.0)))
    return spread * (gradient_size(factor) ** 2 / 19.0)


def draw_doc_ids(key, part):
    key = jax.random.fold_in(key, 11)
    cut_key, late_key, slot_key = jax.random.split(key, 3)
    cut_points = jax.random.randint(cut_key, (SEQS,), 1, SEQ_LEN)
    late_cuts = jax.random.randint(late_key, (SEQS,), SEQ_LEN - TOK_CTX + 1, SEQ_LEN)
    chosen_slot = jax.random.randint(slot_key, (SEQS // SEQ_DEV,), 0, SEQ_DEV)
    is_whole = jnp.repeat(chosen_slot, SEQ_DEV) == jnp.arange(SEQS) % SEQ_DEV
    cut_points = jnp.where(is_whole, late_cuts, cut_points)
    positions = jnp.arange(SEQ_LEN)
    return (positions[None, :] >= cut_points[:, None]).astype(jnp.int32)


def draw_vector_weight(key, part):
    key = jax.random.fold_in(key, 13)
    gain_key, shift_key = jax.random.split(key)
    gains = jax.random.uniform(gain_key, (VEC_ROWS, D), jnp.float32, 0.6, 1.6)
    shifts = jax.random.normal(shift_key, (VEC_ROWS, D), jnp.float32) * 0.3
    row_index = jnp.arange(VEC_ROWS)[:, None]
    return jnp.where((row_index == 0) | (row_index == 2), gains, shifts)


def draw_inward_moment(key, part):
    key = jax.random.fold_in(key, 21)
    return first_entries(key, (D, 3 * D), 1.0)


def draw_inward_square(key, part):
    key = jax.random.fold_in(key, 22)
    return second_entries(key, (D, 3 * D), 1.0)


def draw_outward_moment(key, part):
    key = jax.random.fold_in(key, 23)
    return first_entries(key, (D, D), 0.3)


def draw_outward_square(key, part):
    key = jax.random.fold_in(key, 24)
    return second_entries(key, (D, D), 0.3)


def draw_expand_moment(key, part):
    key = jax.random.fold_in(key, 25)
    return first_entries(key, (D, FF), 0.3)


def draw_expand_square(key, part):
    key = jax.random.fold_in(key, 26)
    return second_entries(key, (D, FF), 0.3)


def draw_shrink_moment(key, part):
    key = jax.random.fold_in(key, 27)
    return first_entries(key, (FF, D), 0.5)


def draw_shrink_square(key, part):
    key = jax.random.fold_in(key, 28)
    return second_entries(key, (FF, D), 0.5)


def draw_vector_moment(key, part):
    key = jax.random.fold_in(key, 29)
    return first_entries(key, (VEC_ROWS, D), 1.0)


def draw_vector_square(key, part):
    key = jax.random.fold_in(key, 30)
    return second_entries(key, (VEC_ROWS, D), 1.0)


def block_levels(rng, dims, shards, smallest, largest):
    level = 1.0
    for axis_at, shards_of in shards:
        draws = jax.random.uniform(jax.random.fold_in(jax.random.fold_in(rng, 6), axis_at), (shards_of,), jnp.float32, smallest / len(shards), largest / len(shards))
        level = level * jnp.repeat(jnp.exp(draws), dims[axis_at] // shards_of).reshape((-1,) + (1,) * (len(dims) - 1 - axis_at))
    return level


def normal_values(stream_key, extent, width, reach, pieces=(), dtype=jnp.bfloat16):
    factor_of = block_levels(stream_key, extent, pieces, -0.22, 0.18) if pieces else 1.0
    entries = jax.random.normal(stream_key, extent, jnp.float32) * width * factor_of
    return jnp.minimum(jnp.maximum(entries, -reach), reach).astype(dtype)


def setup_inputs(seed: int = 0) -> dict:
    seeds = jax.random.split(jax.random.key(seed), 19)
    block_input = normal_values(seeds[0], (SEQS, SEQ_LEN, D), 1.0, 6.0, ((0, 8), (1, 4)))
    doc_ids = draw_doc_ids(jax.random.fold_in(seeds[18], 71), 0)
    out_cotangent = normal_values(seeds[2], (SEQS, SEQ_LEN, D), 1.0, 6.0, ((0, 8), (1, 4)))
    inward_weight = normal_values(seeds[3], (D, 3 * D), (D // 2) ** -0.5, 0.25, ((1, 2),), jnp.float32)
    inward_moment = draw_inward_moment(jax.random.fold_in(seeds[18], 71), 0)
    inward_square = draw_inward_square(jax.random.fold_in(seeds[18], 71), 0)
    outward_weight = normal_values(seeds[6], (D, D), (D // 16) ** -0.5, 0.75, ((1, 2),), jnp.float32)
    outward_moment = draw_outward_moment(jax.random.fold_in(seeds[18], 71), 0)
    outward_square = draw_outward_square(jax.random.fold_in(seeds[18], 71), 0)
    expand_weight = normal_values(seeds[9], (D, FF), D ** -0.5, 0.1875, ((1, 2),), jnp.float32)
    expand_moment = draw_expand_moment(jax.random.fold_in(seeds[18], 71), 0)
    expand_square = draw_expand_square(jax.random.fold_in(seeds[18], 71), 0)
    shrink_weight = normal_values(seeds[12], (FF, D), FF ** -0.5, 0.09375, ((1, 2),), jnp.float32)
    shrink_moment = draw_shrink_moment(jax.random.fold_in(seeds[18], 71), 0)
    shrink_square = draw_shrink_square(jax.random.fold_in(seeds[18], 71), 0)
    vector_weight = draw_vector_weight(jax.random.fold_in(seeds[18], 71), 0)
    vector_moment = draw_vector_moment(jax.random.fold_in(seeds[18], 71), 0)
    vector_square = draw_vector_square(jax.random.fold_in(seeds[18], 71), 0)
    return {"block_input": block_input, "doc_ids": doc_ids, "out_cotangent": out_cotangent, "inward_weight": inward_weight, "inward_moment": inward_moment, "inward_square": inward_square, "outward_weight": outward_weight, "outward_moment": outward_moment, "outward_square": outward_square, "expand_weight": expand_weight, "expand_moment": expand_moment, "expand_square": expand_square, "shrink_weight": shrink_weight, "shrink_moment": shrink_moment, "shrink_square": shrink_square, "vector_weight": vector_weight, "vector_moment": vector_moment, "vector_square": vector_square}


@jax.custom_vjp
def low(v):
    return lax.optimization_barrier(v.astype(jnp.bfloat16)).astype(jnp.float32)

@jax.custom_vjp
def low_back(v):
    return v

def low_keep(v):
    return (low(v), None)

def low_pass(kept, grad):
    return (grad,)

def back_keep(v):
    return (v, None)

def back_low(kept, grad):
    return (low(grad),)
low.defvjp(low_keep, low_pass)
low_back.defvjp(back_keep, back_low)
norm_eps = 1e-05
adam_eps = 1e-08
first_decay = 0.9
second_decay = 0.95
decay_rate = 0.01
matrix_rate = 0.1
vector_rate = 0.8

def layer_norm(values, norm_gain, norm_shift):
    row_mean = lax.optimization_barrier(jnp.mean(values, -1, keepdims=True))
    centred = values - row_mean
    variance = lax.optimization_barrier(jnp.mean(centred * centred, -1, keepdims=True))
    return centred * lax.rsqrt(variance + norm_eps) * norm_gain + norm_shift

def rotary_tables(positions, rot_dims):
    half_rot = rot_dims // 2
    frequency = jnp.exp(jnp.arange(half_rot).astype(jnp.float32) * (-2.0 * math.log(10000.0) / rot_dims))
    angles = positions[:, None] * frequency[None, :]
    angles = jnp.concatenate([angles, angles], -1)
    return (jnp.cos(angles), jnp.sin(angles))

def rotate(values, cosine_table, sine_table):
    rot_dims = cosine_table.shape[-1]
    half_rot = rot_dims // 2
    rot_part = values[..., :rot_dims]
    lower_half = rot_part[..., :half_rot]
    upper_half = rot_part[..., half_rot:]
    turned = jnp.concatenate([-upper_half, lower_half], -1)
    spun = rot_part * cosine_table[:, None, :] + turned * sine_table[:, None, :]
    return jnp.concatenate([spun, values[..., rot_dims:]], -1)

def product(left, right):
    return jnp.einsum('...d,de->...e', left, right, precision=lax.Precision.HIGHEST, preferred_element_type=jnp.float32)

def attend(query, key_low, value_low, allowed):
    group_size, seq_length, head_count, head_size = query.shape
    head_block = math.gcd(head_count, 4)
    block_count = head_count // head_block
    score_scale = head_size ** (-0.5)

    def head_stack(values):
        return values.reshape(group_size, seq_length, block_count, head_block, head_size).transpose(2, 0, 1, 3, 4)

    def one_block(head_parts):
        query_part, key_part, value_part = head_parts
        scores = jnp.einsum('gqhe,gkhe->ghqk', query_part, key_part, precision=lax.Precision.HIGHEST, preferred_element_type=jnp.float32) * score_scale
        scores = jnp.where(allowed[:, None], low_back(scores), -1e+30)
        attn_probs = jax.nn.softmax(scores, axis=-1)
        return jnp.einsum('ghqk,gkhe->gqhe', low(attn_probs), value_part, precision=lax.Precision.HIGHEST, preferred_element_type=jnp.float32)
    stacked = lax.map(jax.checkpoint(one_block), (head_stack(query), head_stack(key_low), head_stack(value_low)))
    return stacked.transpose(1, 2, 0, 3, 4).reshape(group_size, seq_length, head_count * head_size)

def block_layer(weights, group_input, doc_rows, cosine_table, sine_table):
    inward, outward, expand, shrink, vector = weights
    group_size, seq_length, model_width = group_input.shape
    head_size = model_width // HEADS
    ffn_rows = expand.shape[1] // model_width
    normed_attn = layer_norm(group_input, vector[0], vector[1])
    normed_mlp = layer_norm(group_input, vector[2], vector[3])
    joint_rows = low_back(product(low(normed_attn), inward) + vector[4:7].reshape(-1))
    split_shape = (group_size, seq_length, HEADS, head_size)
    query = low(rotate(joint_rows[..., :model_width].reshape(split_shape), cosine_table, sine_table))
    key_low = low(rotate(joint_rows[..., model_width:2 * model_width].reshape(split_shape), cosine_table, sine_table))
    value_low = low(joint_rows[..., 2 * model_width:].reshape(split_shape))
    places = jnp.arange(seq_length)
    causal = places[None, :] <= places[:, None]
    allowed = causal[None] & (doc_rows[:, :, None] == doc_rows[:, None, :])
    attended = low(low_back(attend(query, key_low, value_low, allowed)))
    attn_out = product(attended, outward) + vector[7]
    pre_act = low_back(product(low(normed_mlp), expand) + vector[8:8 + ffn_rows].reshape(-1))
    act_low = low(jax.nn.gelu(pre_act, approximate=False))
    mlp_out = product(act_low, shrink) + vector[8 + ffn_rows]
    return group_input + attn_out + mlp_out

def adam_step(weight, moment, square, gradient, rate):
    first = first_decay * moment + (1.0 - first_decay) * gradient
    second = second_decay * square + (1.0 - second_decay) * gradient * gradient
    first_hat = first / (1.0 - first_decay ** STEP)
    second_hat = second / (1.0 - second_decay ** STEP)
    master = weight - rate * (first_hat / (jnp.sqrt(second_hat) + adam_eps) + decay_rate * weight)
    return (master, first, second)

def reference(block_input, doc_ids, out_cotangent, inward_weight, inward_moment, inward_square, outward_weight, outward_moment, outward_square, expand_weight, expand_moment, expand_square, shrink_weight, shrink_moment, shrink_square, vector_weight, vector_moment, vector_square):
    masters = (inward_weight, outward_weight, expand_weight, shrink_weight, vector_weight)
    pack_size = math.gcd(SEQS, 2)
    grouped_input = block_input.astype(jnp.float32).reshape(SEQS // pack_size, pack_size, SEQ_LEN, D)
    grouped_docs = doc_ids.reshape(SEQS // pack_size, pack_size, SEQ_LEN)
    positions = jnp.arange(SEQ_LEN).astype(jnp.float32)
    cosine_table, sine_table = rotary_tables(positions, ROTARY)

    def forward(master_list, inputs):
        weights_low = tuple((low(weight) for weight in master_list))

        def group_step(weights_carry, group_items):
            group_input, doc_rows = group_items
            return (weights_carry, block_layer(weights_carry, group_input, doc_rows, cosine_table, sine_table))
        _, stacked = lax.scan(jax.checkpoint(group_step), weights_low, (inputs, grouped_docs))
        return stacked
    outputs, pull_back = jax.vjp(forward, masters, grouped_input)
    master_grads, input_grads = pull_back(out_cotangent.astype(jnp.float32).reshape(outputs.shape))
    block_output = outputs.reshape(SEQS, SEQ_LEN, D).astype(jnp.bfloat16)
    input_grad = input_grads.reshape(SEQS, SEQ_LEN, D)
    inward_master, inward_first, inward_second = adam_step(inward_weight, inward_moment, inward_square, master_grads[0], matrix_rate)
    outward_master, outward_first, outward_second = adam_step(outward_weight, outward_moment, outward_square, master_grads[1], matrix_rate)
    expand_master, expand_first, expand_second = adam_step(expand_weight, expand_moment, expand_square, master_grads[2], matrix_rate)
    shrink_master, shrink_first, shrink_second = adam_step(shrink_weight, shrink_moment, shrink_square, master_grads[3], matrix_rate)
    vector_master, vector_first, vector_second = adam_step(vector_weight, vector_moment, vector_square, master_grads[4], vector_rate)
    return (block_output, input_grad, inward_master, inward_first, inward_second, outward_master, outward_first, outward_second, expand_master, expand_first, expand_second, shrink_master, shrink_first, shrink_second, vector_master, vector_first, vector_second)
```

```python
import functools
import math

import jax
import jax.numpy as jnp
from jax import lax
from jax.experimental import pallas as pl
from jax.experimental.pallas import tpu as pltpu
from jax.sharding import PartitionSpec as P

HEADS = 16
ROTARY = 16
STEP = 10


norm_eps = 1e-05
adam_eps = 1e-08
first_decay = 0.9
second_decay = 0.95
decay_rate = 0.01
matrix_rate = 0.1
vector_rate = 0.8
neg_fill = -1e30


def layer_norm(values, norm_gain, norm_shift):
    row_mean = jnp.mean(values, -1, keepdims=True)
    centred = values - row_mean
    variance = jnp.mean(centred * centred, -1, keepdims=True)
    return centred * lax.rsqrt(variance + norm_eps) * norm_gain + norm_shift


def lane_tables(positions, head_size, width):
    half_rot = ROTARY // 2
    lane = jnp.arange(width) % head_size
    frequency = jnp.exp(
        (lane % half_rot).astype(jnp.float32) * (-2.0 * math.log(10000.0) / ROTARY)
    )
    angles = positions[:, None] * frequency[None, :]
    cosine = jnp.where(lane < ROTARY, jnp.cos(angles), 1.0)
    sine = jnp.where(lane < ROTARY, jnp.sin(angles), 0.0)
    return cosine, jnp.where(lane < half_rot, -sine, sine)


def spin(values, cosine, signed_sine):
    half_rot = ROTARY // 2
    width = values.shape[-1]
    lane = lax.broadcasted_iota(jnp.int32, values.shape, 1) % 64
    partner = jnp.where(
        lane < half_rot,
        pltpu.roll(values, width - half_rot, 1),
        pltpu.roll(values, half_rot, 1),
    )
    return values * cosine + partner * signed_sine


def joint_kernel(score_scale, q_blocks, rows_ref, weight_ref, bias_ref, cos_ref, sin_ref, q_ref, kv_ref):
    place = pl.program_id(0)
    tok_count = cos_ref.shape[0]
    seq_count = rows_ref.shape[0] // tok_count
    width = weight_ref.shape[1]
    for seq in range(seq_count):
        span = pl.ds(seq * tok_count, tok_count)
        product = (
            jnp.dot(rows_ref[span, :], weight_ref[...], preferred_element_type=jnp.float32)
            + bias_ref[...]
        )

        @pl.when(place < 2 * q_blocks)
        def _():
            for first in range(0, width, 128):
                turned = spin(product[:, first : first + 128], cos_ref[...], sin_ref[...])

                @pl.when(place < q_blocks)
                def _():
                    low = turned.astype(jnp.bfloat16).astype(jnp.float32) * score_scale
                    q_ref[span, first : first + 128] = low.astype(jnp.bfloat16)

                @pl.when(place >= q_blocks)
                def _():
                    kv_ref[span, first : first + 128] = turned.astype(jnp.bfloat16)

        @pl.when(place >= 2 * q_blocks)
        def _():
            kv_ref[span, :] = product.astype(jnp.bfloat16)


def project_joint(rows, weight, bias, cosine, sine, score_scale):
    row_count, width = rows.shape
    block = 512
    q_blocks = width // block
    whole = lambda j: (0, 0)
    return pl.pallas_call(
        functools.partial(joint_kernel, score_scale, q_blocks),
        grid=(3 * q_blocks,),
        in_specs=[
            pl.BlockSpec((row_count, width), whole),
            pl.BlockSpec((width, block), lambda j: (0, j)),
            pl.BlockSpec((1, block), lambda j: (0, j)),
            pl.BlockSpec(cosine.shape, whole),
            pl.BlockSpec(sine.shape, whole),
        ],
        out_specs=[
            pl.BlockSpec((row_count, block), lambda j: (0, jnp.minimum(j, q_blocks - 1))),
            pl.BlockSpec((row_count, block), lambda j: (0, jnp.maximum(j - q_blocks, 0))),
        ],
        out_shape=[
            jax.ShapeDtypeStruct((row_count, width), jnp.bfloat16),
            jax.ShapeDtypeStruct((row_count, 2 * width), jnp.bfloat16),
        ],
        compiler_params=pltpu.CompilerParams(vmem_limit_bytes=40 * 2**20),
        cost_estimate=pl.CostEstimate(
            flops=6 * row_count * width * width, bytes_accessed=14 * 2**20, transcendentals=0
        ),
        name="joint_projection",
    )(rows, weight, bias, cosine, sine)


def attend_kernel(
    chunk, score_scale, q_ref, k_ref, v_ref, g_ref, low_ref, top_ref, cosk_ref, sink_ref,
    cosq_ref, sinq_ref, out_ref, dq_ref, dk_ref, dv_ref, bias_ref, prob_ref, grad_ref,
):
    key_count = k_ref.shape[1]
    tok_count = q_ref.shape[0]
    chunks = key_count // chunk

    @pl.when(pl.program_id(0) == 0)
    def _():
        for c in range(chunks):
            key_place = c * chunk + lax.broadcasted_iota(jnp.int32, (chunk, tok_count), 0)
            kept = (key_place >= low_ref[0]) & (key_place <= top_ref[...])
            bias_ref[c * chunk : (c + 1) * chunk, :] = jnp.where(kept, 0.0, neg_fill)

    nt = (((1,), (1,)), ((), ()))
    tn = (((0,), (0,)), ((), ()))
    lane = lax.broadcasted_iota(jnp.int32, (tok_count, 128), 1)
    head_row = lax.broadcasted_iota(jnp.int32, (128, tok_count), 0)
    spans = [slice(c * chunk, (c + 1) * chunk) for c in range(chunks)]
    outs, dqs = [], []
    for head in range(2):
        own = (lane // 64) == head
        query = jnp.where(own, q_ref[...], jnp.zeros_like(q_ref))
        grad = jnp.where(own, g_ref[...], jnp.zeros_like(g_ref))
        top = None
        for span in spans:
            scores = (
                lax.dot_general(k_ref[0, span, :], query, nt, preferred_element_type=jnp.float32)
                + bias_ref[span, :]
            )
            prob_ref[head, span, :] = scores
            chunk_top = jnp.max(scores, 0, keepdims=True)
            top = chunk_top if top is None else jnp.maximum(top, chunk_top)
        total = jnp.zeros((1, tok_count), jnp.float32)
        weighted = jnp.zeros((1, tok_count), jnp.float32)
        for span in spans:
            lifted = jnp.exp(prob_ref[head, span, :] - top)
            prob_grad = lax.dot_general(
                v_ref[0, span, :], grad, nt, preferred_element_type=jnp.float32
            )
            prob_ref[head, span, :] = lifted
            grad_ref[head, span, :] = prob_grad
            total += jnp.sum(lifted, 0, keepdims=True)
            weighted += jnp.sum(lifted * prob_grad, 0, keepdims=True)
        inverse = 1.0 / total
        weighted = weighted * inverse
        out = jnp.zeros((128, tok_count), jnp.float32)
        dq = jnp.zeros((128, tok_count), jnp.float32)
        for span in spans:
            probs = prob_ref[head, span, :] * inverse
            probs_low = probs.astype(jnp.bfloat16)
            score_grad = (probs * (grad_ref[head, span, :] - weighted)).astype(jnp.bfloat16)
            out += lax.dot_general(v_ref[0, span, :], probs_low, tn, preferred_element_type=jnp.float32)
            dq += lax.dot_general(k_ref[0, span, :], score_grad, tn, preferred_element_type=jnp.float32)
            dv = jnp.dot(probs_low, grad, preferred_element_type=jnp.float32)
            dk = jnp.dot(score_grad, query, preferred_element_type=jnp.float32)
            dk = spin(dk, cosk_ref[span, :], -sink_ref[span, :])
            key_lane = lax.broadcasted_iota(jnp.int32, dk.shape, 1)
            if head == 0:
                dv_ref[span, :] = dv.astype(jnp.bfloat16)
                dk_ref[span, :] = dk.astype(jnp.bfloat16)
            else:
                dv_ref[span, :] = jnp.where(key_lane < 64, dv_ref[span, :], dv.astype(jnp.bfloat16))
                dk_ref[span, :] = jnp.where(key_lane < 64, dk_ref[span, :], dk.astype(jnp.bfloat16))
        outs.append(out)
        dqs.append(dq)
    out_ref[...] = jnp.where(head_row < 64, outs[0], outs[1]).T.astype(jnp.bfloat16)
    dq = jnp.where(head_row < 64, dqs[0], dqs[1]).T * score_scale
    dq_ref[...] = spin(dq, cosq_ref[...], -sinq_ref[...]).astype(jnp.bfloat16)


def attend(seq, query, kv, grad, lows, tops, key_tables, query_tables, score_scale):
    tok_count = tops.shape[1]
    width = query.shape[1]
    key_count = kv.shape[1]
    pairs = width // 128
    whole = lambda j: (0, 0)
    columns = lambda j: (0, j)
    own = lambda j: (seq, j)
    return pl.pallas_call(
        functools.partial(attend_kernel, 512, score_scale),
        grid=(pairs,),
        in_specs=[
            pl.BlockSpec((tok_count, 128), own),
            pl.BlockSpec((1, key_count, 128), lambda j: (seq, 0, j)),
            pl.BlockSpec((1, key_count, 128), lambda j: (seq, 0, pairs + j)),
            pl.BlockSpec((tok_count, 128), own),
            pl.BlockSpec((1, 1, tok_count), lambda j: (seq, 0, 0)),
            pl.BlockSpec((1, tok_count), whole),
            pl.BlockSpec((key_count, 128), whole),
            pl.BlockSpec((key_count, 128), whole),
            pl.BlockSpec((tok_count, 128), whole),
            pl.BlockSpec((tok_count, 128), whole),
        ],
        out_specs=[
            pl.BlockSpec((tok_count, 128), columns),
            pl.BlockSpec((tok_count, 128), columns),
            pl.BlockSpec((key_count, 128), columns),
            pl.BlockSpec((key_count, 128), columns),
        ],
        out_shape=[
            jax.ShapeDtypeStruct((tok_count, width), jnp.bfloat16),
            jax.ShapeDtypeStruct((tok_count, width), jnp.bfloat16),
            jax.ShapeDtypeStruct((key_count, width), jnp.bfloat16),
            jax.ShapeDtypeStruct((key_count, width), jnp.bfloat16),
        ],
        scratch_shapes=[
            pltpu.VMEM((key_count, tok_count), jnp.float32),
            pltpu.VMEM((2, key_count, tok_count), jnp.float32),
            pltpu.VMEM((2, key_count, tok_count), jnp.float32),
        ],
        compiler_params=pltpu.CompilerParams(vmem_limit_bytes=56 * 2**20),
        cost_estimate=pl.CostEstimate(
            flops=100 * 10**9, bytes_accessed=20 * 2**20, transcendentals=pairs * 2 * key_count * tok_count
        ),
        name="attention_both_ways",
    )(query, kv, kv, grad, lows, tops, *key_tables, *query_tables)


def gelu_exact(values):
    return jax.nn.gelu(values, approximate=False)


def gather_weight(weight):
    rows = weight.shape[0] // lax.axis_size("ctx")
    part = lax.dynamic_slice_in_dim(weight, lax.axis_index("ctx") * rows, rows, 0)
    part = lax.all_gather(part.astype(jnp.bfloat16), "group", axis=1, tiled=True)
    return lax.all_gather(part, "ctx", axis=0, tiled=True)


def reduce_gradient(gradient):
    part = lax.psum_scatter(gradient, ("ctx", "batch"), scatter_dimension=0, tiled=True)
    part = lax.psum_scatter(part, "group", scatter_dimension=1, tiled=True)
    return lax.all_gather(part, ("ctx", "batch"), axis=0, tiled=True)


def adam_step(weight, moment, square, gradient, rate):
    first = first_decay * moment + (1.0 - first_decay) * gradient
    second = second_decay * square + (1.0 - second_decay) * gradient * gradient
    first_hat = first / (1.0 - first_decay**STEP)
    second_hat = second / (1.0 - second_decay**STEP)
    master = weight - rate * (first_hat / (jnp.sqrt(second_hat) + adam_eps) + decay_rate * weight)
    return (master, first, second)


def update_all(weights, moments, squares, gradients):
    rates = (matrix_rate, matrix_rate, matrix_rate, matrix_rate, vector_rate)
    results = ()
    for place in range(5):
        results = results + adam_step(
            weights[place], moments[place], squares[place], gradients[place], rates[place]
        )
    return results


def local(
    block_input,
    doc_ids,
    out_cotangent,
    inward_weight,
    inward_moment,
    inward_square,
    outward_weight,
    outward_moment,
    outward_square,
    expand_weight,
    expand_moment,
    expand_square,
    shrink_weight,
    shrink_moment,
    shrink_square,
    vector_weight,
    vector_moment,
    vector_square,
):
    vector_full = lax.all_gather(
        vector_weight.astype(jnp.bfloat16), "group", axis=1, tiled=True
    ).astype(jnp.float32)
    inward_copy = gather_weight(inward_weight)
    expand_copy = gather_weight(expand_weight)
    shrink_copy = gather_weight(shrink_weight)
    outward_copy = gather_weight(outward_weight)
    seq_count, tok_count, model_width = block_input.shape
    head_size = model_width // HEADS
    seq_length = doc_ids.shape[1]
    ffn_rows = expand_copy.shape[1] // model_width
    row_count = seq_count * tok_count
    score_scale = head_size ** (-0.5)
    offset = lax.axis_index("ctx") * tok_count
    residual = block_input.astype(jnp.float32).reshape(row_count, model_width)
    normed_attn, attn_norm_back = jax.vjp(layer_norm, residual, vector_full[0], vector_full[1])
    normed_mlp, mlp_norm_back = jax.vjp(layer_norm, residual, vector_full[2], vector_full[3])
    attn_in = normed_attn.astype(jnp.bfloat16)
    mlp_in = normed_mlp.astype(jnp.bfloat16)
    key_tables = lane_tables(jnp.arange(seq_length).astype(jnp.float32), head_size, 128)
    query_places = offset + jnp.arange(tok_count)
    query_tables = lane_tables(query_places.astype(jnp.float32), head_size, 128)
    query_low, kv_low = project_joint(
        attn_in, inward_copy, vector_full[4:7].reshape(1, -1), *query_tables, score_scale
    )
    kv_rows = lax.all_gather(
        kv_low.reshape(seq_count, tok_count, 2 * model_width), "ctx", axis=1, tiled=True
    )
    own_docs = lax.dynamic_slice_in_dim(doc_ids, offset, tok_count, 1)
    cut = jnp.sum((doc_ids == 0).astype(jnp.int32), 1, keepdims=True)
    lows = jnp.where(own_docs == 0, 0, cut)[:, None, :]
    tops = query_places.astype(jnp.int32)[None, :]
    pre_act = jnp.dot(mlp_in, expand_copy, preferred_element_type=jnp.float32) + vector_full[
        8 : 8 + ffn_rows
    ].reshape(-1)
    activation, act_back = jax.vjp(gelu_exact, pre_act)
    act_low = activation.astype(jnp.bfloat16)
    grad_low = out_cotangent.reshape(row_count, model_width)
    grad_out = grad_low.astype(jnp.float32)
    shrink_grad = jnp.dot(act_low.T, grad_low, preferred_element_type=jnp.float32).astype(
        jnp.bfloat16
    )
    act_grad = jnp.dot(grad_low, shrink_copy.T, preferred_element_type=jnp.float32)
    pre_grad = act_back(act_grad)[0].astype(jnp.bfloat16)
    expand_grad = jnp.dot(mlp_in.T, pre_grad, preferred_element_type=jnp.float32).astype(
        jnp.bfloat16
    )
    attended_grad = jnp.dot(grad_low, outward_copy.T, preferred_element_type=jnp.float32).astype(
        jnp.bfloat16
    )
    shrink_grad, expand_grad, attended_grad = lax.optimization_barrier(
        (shrink_grad, expand_grad, attended_grad)
    )
    attended, query_grads, key_grads, value_grads = [], [], [], []
    for seq in range(seq_count):
        out, dq, dk, dv = attend(
            seq, query_low, kv_rows, attended_grad, lows, tops, key_tables, query_tables, score_scale
        )
        attended.append(out)
        query_grads.append(dq)
        key_grads.append(lax.psum_scatter(dk, "ctx", scatter_dimension=0, tiled=True))
        value_grads.append(lax.psum_scatter(dv, "ctx", scatter_dimension=0, tiled=True))
    attn_low = jnp.concatenate(attended, 0)
    outward_grad = jnp.dot(attn_low.T, grad_low, preferred_element_type=jnp.float32).astype(
        jnp.bfloat16
    )
    attn_out = jnp.dot(attn_low, outward_copy, preferred_element_type=jnp.float32) + vector_full[7]
    mlp_out = (
        jnp.dot(act_low, shrink_copy, preferred_element_type=jnp.float32)
        + vector_full[8 + ffn_rows]
    )
    block_output = (
        (residual + attn_out + mlp_out)
        .astype(jnp.bfloat16)
        .reshape(seq_count, tok_count, model_width)
    )
    mlp_in_grad = jnp.dot(pre_grad, expand_copy.T, preferred_element_type=jnp.float32)
    joint_grad = jnp.concatenate(
        [
            jnp.concatenate(query_grads, 0),
            jnp.concatenate(key_grads, 0),
            jnp.concatenate(value_grads, 0),
        ],
        -1,
    )
    inward_grad = jnp.dot(attn_in.T, joint_grad, preferred_element_type=jnp.float32).astype(
        jnp.bfloat16
    )
    attn_in_grad = jnp.dot(joint_grad, inward_copy.T, preferred_element_type=jnp.float32)
    residual_attn, gain_attn, shift_attn = attn_norm_back(attn_in_grad)
    residual_mlp, gain_mlp, shift_mlp = mlp_norm_back(mlp_in_grad)
    input_grad = (grad_out + residual_attn + residual_mlp).reshape(
        seq_count, tok_count, model_width
    )
    joint_sum = jnp.sum(joint_grad.astype(jnp.float32), 0).reshape(3, model_width)
    out_sum = jnp.sum(grad_out, 0)
    pre_sum = jnp.sum(pre_grad.astype(jnp.float32), 0).reshape(ffn_rows, model_width)
    vector_grad = jnp.concatenate(
        [
            gain_attn[None],
            shift_attn[None],
            gain_mlp[None],
            shift_mlp[None],
            joint_sum,
            out_sum[None],
            pre_sum,
            out_sum[None],
        ],
        0,
    )
    vector_sum = lax.psum(vector_grad, ("batch", "group", "ctx"))
    own_width = vector_weight.shape[1]
    vector_own = lax.dynamic_slice_in_dim(
        vector_sum, lax.axis_index("group") * own_width, own_width, 1
    )
    masters = (inward_weight, outward_weight, expand_weight, shrink_weight, vector_weight)
    moments = (inward_moment, outward_moment, expand_moment, shrink_moment, vector_moment)
    squares = (inward_square, outward_square, expand_square, shrink_square, vector_square)
    summed = tuple(
        reduce_gradient(gradient).astype(jnp.float32)
        for gradient in (inward_grad, outward_grad, expand_grad, shrink_grad)
    ) + (vector_own,)
    results = update_all(masters, moments, squares, summed)
    return (block_output, input_grad) + tuple(results)


def solution(mesh):
    placed = (
        P(("batch", "group"), "ctx", None),
        P(("batch", "group"), None),
        P(("batch", "group"), "ctx", None),
        P(None, "group"),
        P(None, "group"),
        P(None, "group"),
        P(None, "group"),
        P(None, "group"),
        P(None, "group"),
        P(None, "group"),
        P(None, "group"),
        P(None, "group"),
        P(None, "group"),
        P(None, "group"),
        P(None, "group"),
        P(None, "group"),
        P(None, "group"),
        P(None, "group"),
    )
    return jax.shard_map(
        local,
        mesh=mesh,
        in_specs=placed,
        out_specs=(
            P(("batch", "group"), "ctx", None),
            P(("batch", "group"), "ctx", None),
            P(None, "group"),
            P(None, "group"),
            P(None, "group"),
            P(None, "group"),
            P(None, "group"),
            P(None, "group"),
            P(None, "group"),
            P(None, "group"),
            P(None, "group"),
            P(None, "group"),
            P(None, "group"),
            P(None, "group"),
            P(None, "group"),
            P(None, "group"),
            P(None, "group"),
        ),
        check_vma=False,
    )
```
